32 devices in a mesh: groups: 2 (over x), expert: 16 (over z, y, core).
Axes of the slice: x: 2, y: 2, z: 4, core: 2. Of those that a mesh axis runs over, the one named last changes fastest.
Arguments:
- cotangent: bfloat16 [4096, 4096], P(('groups', 'expert')), parts along dimension 0, may hold values from -6 to 6
- expert_ids: int32 [4096, 8], P(('groups', 'expert')), parts along dimension 0, may hold values from 0 to 15, all different within a row; in each aligned block of 128 rows (0 to 127, 128 to 255, ...) at most 80 rows name the same one
- gate_probs: bfloat16 [4096, 8], P(('groups', 'expert')), parts along dimension 0, may hold values from 0.019897461 to 0.5
- seq_ids: int32 [4096], P(('groups', 'expert')), parts along dimension 0, may hold values from 0 to 1, never falling along the last dimension, each value on 1 to 2047 neighbouring positions
- hidden_saved: bfloat16 [32, 1280, 768], P(('groups', 'expert')), parts along dimension 0, may hold values from -2 to 2
Outputs:
- fisher: bfloat16 [32, 768, 4096], P(('groups', 'expert')), parts along dimension 0
The draws below stay inside these ranges and needn't reach their ends.
There are 2 independent parts, one for each index of `groups`. The reference program is written for one: setup_inputs(seed, part) draws one part's arguments, and reference() takes and returns one part's arrays. A program takes and returns all parts, laid end to end along the dimension named above; each array names one. Nothing has to cross between parts.
Inputs may be any that keep to these rules, and one draw needn't show every extreme that they name: `expert_ids`: each row names 8 different experts; among the 128 tokens of one device no expert is named more than 80 times, and this bound is reached. `seq_ids`: never falling along the tokens; each sequence has 1 to 2047 tokens.
All inputs are finite; a program needn't handle non-finite values.
Results may differ from the reference program's by a relative error of at most 0.0052.
Values may be sent and summed in bfloat16 or wider, within the bound.
A program may use at most 128 MiB of HBM per device.

```python
import math
import jax
import jax.numpy as jnp
import numpy as np
from jax import lax

D = 4096
FFW = 768
TOP = 8
TOK_DEV = 128
EXPERTS = 16
TOKENS = 2048
NSEQ = 2
SEQ_MOST = 2047
MOST = 80
WIN = 16
N_EXPERT = 16


def block_levels(rng, shape, split, low, high):
    def one(axis_at, shards_of):
        heights = jax.random.uniform(jax.random.fold_in(jax.random.fold_in(rng, 6), axis_at), (shards_of,), jnp.float32, low / len(split), high / len(split))
        return jnp.repeat(jnp.exp(heights), shape[axis_at] // shards_of).reshape((-1,) + (1,) * (len(shape) - axis_at - 1))

    factor_of = one(*split[0])
    for cut in split[1:]:
        factor_of = factor_of * one(*cut)
    return factor_of


def profile(count, total, limit, lean):
    portions = [(1 << 20) // math.isqrt(standing ** lean) + 1 for standing in range(2, count + 1)]
    rest, counts = total - limit - (count - 1), [1] * (count - 1)
    while rest > 0:
        movable = [i for i in range(count - 1) if counts[i] < limit]
        mass, budget = sum([portions[i] for i in movable]), rest
        for i in movable:
            extra = min(limit - counts[i], max(1, budget * portions[i] // mass), rest)
            counts[i] = counts[i] + extra
            rest = rest - extra
    return np.array([limit] + counts)


def uneven(key, amount, total, bound, slope):
    if amount == 2:
        one = jax.random.randint(key, (), max(1, total - bound), min(bound, total - 1) + 1)
        return jnp.stack([one, total - one])
    sizes = jnp.asarray(profile(amount, total, bound, slope), jnp.int32)
    twos = (amount - 1) // 2
    donor, receiver = sizes[1:1 + 2 * twos:2], sizes[2:2 + 2 * twos:2]
    slack = jnp.minimum(donor - 1, bound - receiver)
    moved = jax.random.randint(jax.random.fold_in(key, 1), (twos,), 0, 1 << 20) % (slack + 1)
    sizes = sizes.at[1:1 + 2 * twos:2].set(donor - moved).at[2:2 + 2 * twos:2].set(receiver + moved)
    return sizes[jax.random.permutation(jax.random.fold_in(key, 2), amount)]


def routed_block(own_key, own, number, rows, amount, top, most, slope):
    ranking = jax.random.permutation(own_key, amount)
    packed, common = load_shares(amount, rows * top, most, slope, True), load_shares(amount, rows * top, most, slope, False)
    places = jnp.arange(amount)

    def named(sizes, turn):
        used = int((sizes > 0).sum())
        fixed = max(1, used // 4)
        shifted = fixed + (places - fixed + turn * (used - fixed)) % max(1, amount - fixed)
        return jnp.zeros((amount,), jnp.int32).at[ranking[jnp.where(places < fixed, places, shifted)]].set(jnp.asarray(sizes, jnp.int32))

    sizes = jnp.where(number % 4 == 0, named(packed, number // 4), named(common, number - number // 4 - 1))
    mixed = jax.random.permutation(jax.random.fold_in(own, 3), amount)
    donor, sink = mixed[0:amount // 2 * 2:2], mixed[1:amount // 2 * 2:2]
    margin = jnp.minimum(sizes[donor] - 1, most - sizes[sink]) // 2
    margin = jnp.where((donor == ranking[0]) | (sink == ranking[0]) | (sizes[sink] == 0), 0, jnp.maximum(margin, 0))
    shifted = jax.random.randint(jax.random.fold_in(own, 4), (amount // 2,), 0, 1 << 20) % (margin + 1)
    sizes = sizes.at[donor].add(-shifted).at[sink].add(shifted)
    labels = jnp.searchsorted(jnp.cumsum(sizes), jnp.arange(rows * top), side="right").astype(jnp.int32)
    table = labels.reshape(top, rows).T
    table = table[jax.random.permutation(jax.random.fold_in(own, 1), rows)]
    turn = jax.random.randint(jax.random.fold_in(own, 2), (rows, 1), 0, top)
    return jnp.take_along_axis(table, (jnp.arange(top)[None, :] + turn) % top, axis=1)


def load_shares(count, total, limit, slope, full):
    portions = [(1 << 20) // math.isqrt(rank ** slope) + 1 for rank in range(1, count + 1)]
    largest = limit if full else min(limit, max(-(-total // count), total * portions[0] // sum(portions)))
    least = 1 if total - largest >= count - 1 else 0
    holding, spare = [largest] + [least] * (count - 1), total - largest - least * (count - 1)
    while spare > 0:
        movable = [i for i in range(1, count) if holding[i] < largest] or [i for i in range(1, count) if holding[i] < limit]
        pool, left = sum([portions[i] for i in movable]), spare
        for i in movable:
            extra = min(limit - holding[i], max(1, left * portions[i] // pool), spare)
            holding[i] = holding[i] + extra
            spare = spare - extra
    return np.array(holding)


def gaussian(stream_key, dims, width, most, shards=(), kind=jnp.bfloat16):
    level = block_levels(stream_key, dims, shards, -0.22, 0.18) if shards else 1.0
    drawn = jax.random.normal(stream_key, dims, jnp.float32) * width * level
    return jnp.minimum(jnp.maximum(drawn, -most), most).astype(kind)


def setup_inputs(seed: int = 0, part: int = 0) -> dict:
    seeds = jax.random.split(jax.random.key(seed), 6)
    part_splits = jax.random.split(jax.random.fold_in(seeds[5], part), 6)
    cotangent = gaussian(part_splits[0], (TOKENS, D), 1.0, 6.0, ((0, 16),))
    expert_ids_keys = jax.random.split(jax.random.fold_in(part_splits[1], 1), TOKENS // TOK_DEV)
    expert_ids_turns = jax.random.permutation(jax.random.fold_in(part_splits[1], 3), TOKENS // TOK_DEV)
    expert_ids = jax.vmap(lambda own, number: routed_block(jax.random.fold_in(part_splits[1], 2), own, number, TOK_DEV, EXPERTS, TOP, MOST, 2))(expert_ids_keys, expert_ids_turns).reshape((TOKENS, TOP))
    gate_probs = jnp.clip(jnp.exp(math.log(0.5) - 3.224016 * jax.random.uniform(part_splits[2], (TOKENS, TOP), jnp.float32) ** block_levels(part_splits[2], (TOKENS, TOP), ((0, 16),), -0.2, 0.2)), 0.019897461, 0.5).astype(jnp.bfloat16)
    seq_ids = jnp.searchsorted(jnp.cumsum(uneven(part_splits[3], NSEQ, TOKENS, SEQ_MOST, 1)), jnp.arange(TOKENS), side="right").astype(jnp.int32)
    hidden_saved = gaussian(part_splits[4], (EXPERTS, N_EXPERT * MOST, FFW), 0.25, 2.0, ((0, 16),))
    return {"cotangent": cotangent, "expert_ids": expert_ids, "gate_probs": gate_probs, "seq_ids": seq_ids, "hidden_saved": hidden_saved}


def build_tables(expert_ids, seq_ids, owner, owners, tok_dev, cap_rows):
    routed = expert_ids == owner
    is_routed = jnp.any(routed, axis=1)
    which_pick = jnp.sum(routed.astype(jnp.int32) * jnp.arange(expert_ids.shape[1], dtype=jnp.int32)[None, :], axis=1)
    per_block = is_routed.astype(jnp.int32).reshape(owners, tok_dev)
    arrival = jnp.cumsum(per_block, axis=1) - per_block
    slot_index = jnp.where(per_block > 0, arrival, cap_rows).astype(jnp.int32)
    source_index = jnp.broadcast_to(jnp.arange(owners, dtype=jnp.int32)[:, None], (owners, tok_dev))
    token_index = jnp.arange(owners * tok_dev, dtype=jnp.int32).reshape(owners, tok_dev)
    token_table = jnp.zeros((owners, cap_rows + 1), jnp.int32).at[source_index, slot_index].set(token_index)
    seq_table = jnp.full((owners, cap_rows + 1), -1, jnp.int32).at[source_index, slot_index].set(seq_ids.reshape(owners, tok_dev).astype(jnp.int32))
    pick_table = jnp.zeros((owners, cap_rows + 1), jnp.int32).at[source_index, slot_index].set(which_pick.reshape(owners, tok_dev).astype(jnp.int32))
    return token_table[:, :cap_rows], seq_table[:, :cap_rows], pick_table[:, :cap_rows]


def fisher_columns(arrived, hidden_rows, seq_table, seq_count, window):
    owners, cap_rows = seq_table.shape
    flat_rows = arrived.reshape(owners * cap_rows, arrived.shape[-1])
    flat_seq = seq_table.reshape(-1)
    block_last = lax.cummax(jnp.max(seq_table, axis=1), axis=0)
    span = window * cap_rows

    def one_sequence(sequence, totals):
        first_block = jnp.sum((block_last < sequence).astype(jnp.int32))
        offset = (first_block * cap_rows).astype(jnp.int32)
        hidden_part = lax.dynamic_slice_in_dim(hidden_rows, offset, span, 0)
        row_part = lax.dynamic_slice_in_dim(flat_rows, offset, span, 0)
        seq_part = lax.dynamic_slice_in_dim(flat_seq, offset, span, 0)
        chosen = jnp.where((seq_part == sequence)[:, None], hidden_part, jnp.zeros_like(hidden_part))
        grad_part = lax.dot_general(chosen, row_part, (((0,), (0,)), ((), ())), preferred_element_type=jnp.float32)
        return totals + grad_part * grad_part

    empty = jnp.zeros((hidden_rows.shape[1], arrived.shape[-1]), jnp.float32)
    totals = lax.fori_loop(0, seq_count, one_sequence, empty)
    return totals.astype(jnp.bfloat16)


def reference(cotangent, expert_ids, gate_probs, seq_ids, hidden_saved):
    def per_owner(owner):
        token_table, seq_table, pick_table = build_tables(expert_ids, seq_ids, owner, N_EXPERT, TOK_DEV, MOST)
        weights = gate_probs[token_table, pick_table].astype(jnp.float32)
        scaled = weights[..., None] * cotangent[token_table].astype(jnp.float32)
        scaled = jnp.where((seq_table >= 0)[..., None], scaled, jnp.zeros_like(scaled)).astype(jnp.bfloat16)
        return fisher_columns(scaled, hidden_saved[owner], seq_table, NSEQ, WIN)

    return lax.map(per_owner, jnp.arange(EXPERTS, dtype=jnp.int32))
```

```python
import functools

import jax
import jax.numpy as jnp
from jax import lax
from jax.experimental import pallas as pl
from jax.experimental.pallas import tpu as pltpu
from jax.sharding import PartitionSpec as P

SEQ_AVG = 8192
CHUNKS = 8


def fisher_columns(arrived, hidden_rows, seq_table, seq_count, window):
    owners, cap_rows = seq_table.shape
    flat_rows = arrived.reshape(owners * cap_rows, arrived.shape[-1])
    flat_seq = seq_table.reshape(-1)
    block_last = lax.cummax(jnp.max(seq_table, axis=1), axis=0)
    span = window * cap_rows

    def one_sequence(sequence, totals):
        first_block = jnp.sum((block_last < sequence).astype(jnp.int32))
        offset = first_block * cap_rows
        hidden_part = lax.dynamic_slice_in_dim(hidden_rows, offset, span, 0)
        row_part = lax.dynamic_slice_in_dim(flat_rows, offset, span, 0)
        seq_part = lax.dynamic_slice_in_dim(flat_seq, offset, span, 0)
        chosen = jnp.where(
            (seq_part == sequence)[:, None], hidden_part, jnp.zeros_like(hidden_part)
        )
        grad_part = lax.dot_general(
            chosen, row_part, (((0,), (0,)), ((), ())), preferred_element_type=jnp.float32
        )
        return totals + grad_part * grad_part

    empty = jnp.zeros((hidden_rows.shape[1], arrived.shape[-1]), jnp.float32)
    totals = lax.fori_loop(0, seq_count, one_sequence, empty)
    return totals.astype(jnp.bfloat16)


def shards(cotangent, expert_ids, gate_probs, seq_ids, hidden_saved):
    owners = lax.axis_size("expert")
    tok_dev = expert_ids.shape[0]
    cap_rows = hidden_saved.shape[1] // owners
    total_tokens = tok_dev * owners
    seq_count = total_tokens // SEQ_AVG + 2
    seq_longest = min(SEQ_AVG * 9 // 8, total_tokens - seq_count + 1)
    window = min(seq_longest // tok_dev + 2, owners)
    expert_iota = jnp.arange(owners, dtype=jnp.int32)
    per_expert = jnp.sum(
        (expert_ids[:, :, None] == expert_iota[None, None, :]).astype(jnp.int32), axis=1
    )
    arrival = jnp.cumsum(per_expert, axis=0) - per_expert
    pair_rank = jnp.take_along_axis(arrival, expert_ids, axis=1)
    pair_slot = expert_ids * cap_rows + pair_rank
    slot_iota = jnp.arange(owners * cap_rows, dtype=jnp.int32)
    placed = slot_iota[:, None, None] == pair_slot[None, :, :]
    weights = jnp.where(placed, gate_probs.astype(jnp.float32)[None, :, :], 0.0)
    dispatch = jnp.sum(weights, axis=2).astype(jnp.bfloat16)
    outgoing = jnp.dot(dispatch, cotangent, preferred_element_type=jnp.float32).astype(jnp.bfloat16)
    outgoing = outgoing.reshape(owners, cap_rows, cotangent.shape[1])
    seq_spread = jnp.broadcast_to(seq_ids[:, None], expert_ids.shape)
    outgoing_seq = (
        jnp.full((owners, cap_rows), -1, jnp.int32).at[expert_ids, pair_rank].set(seq_spread)
    )
    seq_table = lax.all_to_all(outgoing_seq, "expert", split_axis=0, concat_axis=0, tiled=True)
    hidden_rows = hidden_saved[0]
    fisher = fisher_columns(
        lax.all_to_all(outgoing, "expert", split_axis=0, concat_axis=0, tiled=True),
        hidden_rows,
        seq_table,
        seq_count,
        window,
    )
    return fisher[None]


MESH = pl.DeviceIdType.MESH
UP, DOWN, ACROSS, SIBLING = range(4)


def gather_kernel(
    layers, cap_rows, seq_count, chunks,
    cot_ref, meta_ref, hidden_ref, out_ref,
    rows_all, meta_all, hidden_buf, hidden_t, pick_w, slot_rows, stage,
    own_sem, hidden_sem, out_sem, send_sem, recv_sem, meta_send, meta_recv,
):
    places = 2 * layers
    tok_dev, width = rows_all.shape[3:]
    ffw = hidden_t.shape[0]
    me = lax.axis_index("expert")
    core = lax.rem(me, 2)
    place = me // 2
    y = lax.rem(place, 2)
    z = place // 2
    has_up, has_down = z < layers - 1, z > 0
    device = {UP: me + 4, DOWN: me - 4, ACROSS: me + 2 - 4 * y, SIBLING: me + 1 - 2 * core}

    def own_copy(c):
        columns = pl.ds(pl.multiple_of(c * width, width), width)
        return pltpu.make_async_copy(cot_ref.at[:, columns], rows_all.at[c, core, place], own_sem.at[c])

    def rows_copy(c, plane, origin, way):
        return pltpu.make_async_remote_copy(
            src_ref=rows_all.at[c, plane, origin],
            dst_ref=rows_all.at[c, plane, origin],
            send_sem=send_sem.at[c, origin, way],
            recv_sem=recv_sem.at[c, plane, origin],
            device_id={"expert": device[way]},
            device_id_type=MESH,
        )

    def meta_copy(plane, origin, way):
        return pltpu.make_async_remote_copy(
            src_ref=meta_all.at[plane, origin],
            dst_ref=meta_all.at[plane, origin],
            send_sem=meta_send.at[origin, way],
            recv_sem=meta_recv.at[plane, origin],
            device_id={"expert": device[way]},
            device_id_type=MESH,
        )

    def out_copy(c):
        columns = pl.ds(pl.multiple_of(c * width, width), width)
        slot = lax.rem(c, 2)
        return pltpu.make_async_copy(stage.at[slot], out_ref.at[0, :, columns], out_sem.at[slot])

    def send(c, origin, ways):
        @pl.when(c == 0)
        def _():
            for way in ways:
                meta_copy(core, origin, way).start()

        for way in ways:
            rows_copy(c, core, origin, way).start()

    def arrive(c, plane, origin):
        @pl.when(c == 0)
        def _():
            meta_copy(plane, origin, SIBLING).wait_recv()

        rows_copy(c, plane, origin, SIBLING).wait_recv()

    hidden_copy = pltpu.make_async_copy(hidden_ref.at[0], hidden_buf, hidden_sem)
    for c in range(chunks):
        own_copy(c).start()
    hidden_copy.start()
    meta_all[core, place] = meta_ref[...]

    barrier = pltpu.get_barrier_semaphore()
    for way in (ACROSS, SIBLING):
        pl.semaphore_signal(barrier, inc=1, device_id={"expert": device[way]}, device_id_type=MESH)
    for way, there in ((UP, has_up), (DOWN, has_down)):
        @pl.when(there)
        def _():
            pl.semaphore_signal(barrier, inc=1, device_id={"expert": device[way]}, device_id_type=MESH)
    pl.semaphore_wait(barrier, 2 + has_up.astype(jnp.int32) + has_down.astype(jnp.int32))

    def start_own(c):
        own_copy(c).wait()

        @pl.when(has_up)
        def _():
            send(c, place, (UP,))

        @pl.when(has_down)
        def _():
            send(c, place, (DOWN,))

        send(c, place, (ACROSS, SIBLING))

    def relay(c, hop):
        for source, there, onward, way in (
            (z - hop, z >= hop, has_up, UP),
            (z + hop, z + hop < layers, has_down, DOWN),
        ):
            @pl.when(there)
            def _():
                origin = source * 2 + y
                arrive(c, core, origin)

                @pl.when(onward)
                def _():
                    send(c, origin, (way,))

                send(c, origin, (ACROSS, SIBLING))

    def from_across(c):
        for layer in range(layers):
            origin = layer * 2 + 1 - y
            arrive(c, core, origin)
            send(c, origin, (SIBLING,))

    def transpose_hidden():
        hidden_copy.wait()

        def one(i, _):
            rows = pl.ds(pl.multiple_of(i * 128, 128), 128)
            hidden_t[:, rows] = hidden_buf[rows, :].T
            return 0

        lax.fori_loop(0, hidden_buf.shape[0] // 128, one, 0)

    def prepare():
        earlier = lax.broadcasted_iota(jnp.int32, (tok_dev, tok_dev), 0) < lax.broadcasted_iota(
            jnp.int32, (tok_dev, tok_dev), 1
        )
        earlier = earlier.astype(jnp.float32).astype(jnp.bfloat16)
        slots = lax.broadcasted_iota(jnp.int32, (cap_rows, tok_dev), 0).astype(jnp.float32)
        expert = me.astype(jnp.float32)
        top = meta_all.shape[2] // 3
        for plane in range(2):
            table = meta_all[plane]
            named = table[:, :top, :] == expert
            routed = jnp.sum(jnp.where(named, 1.0, 0.0), axis=1)
            gate = jnp.sum(jnp.where(named, table[:, top:2 * top, :], 0.0), axis=1)
            rank = jnp.dot(routed.astype(jnp.bfloat16), earlier, preferred_element_type=jnp.float32)
            for origin in range(places):
                here = routed[origin:origin + 1] > 0
                sequence = table[origin, 2 * top:2 * top + 1, :]
                for s in range(seq_count):
                    spot = jnp.where(here & (sequence == float(s)), rank[origin:origin + 1], -1.0)
                    weight = jnp.where(slots == spot, gate[origin:origin + 1], 0.0)
                    pick_w[plane, origin, s * cap_rows:(s + 1) * cap_rows, :] = weight.astype(jnp.bfloat16)

    def finish(c):
        for origin in range(places):
            arrive(c, 1 - core, origin)

        @pl.when(c == 0)
        def _():
            prepare()

        def dispatch(origin, _):
            for plane in range(2):
                sent = jnp.dot(
                    pick_w[plane, origin], rows_all[c, plane, origin], preferred_element_type=jnp.float32
                ).astype(jnp.bfloat16)
                first = pl.multiple_of((origin * 2 + plane) * cap_rows, 16)
                for s in range(seq_count):
                    slot_rows[s, pl.ds(first, cap_rows), :] = sent[s * cap_rows:(s + 1) * cap_rows]
            return 0

        lax.fori_loop(0, places, dispatch, 0)

        @pl.when(c >= 2)
        def _():
            out_copy(c - 2).wait()

        slot = lax.rem(c, 2)
        tall = 256

        def squares(m, _):
            part = pl.ds(pl.multiple_of(m * tall, tall), tall)
            total = None
            for s in range(seq_count):
                grad = jnp.dot(hidden_t[part, :], slot_rows[s], preferred_element_type=jnp.float32)
                total = grad * grad if total is None else total + grad * grad
            stage[slot, part, :] = total.astype(jnp.bfloat16)
            return 0

        lax.fori_loop(0, ffw // tall, squares, 0)
        out_copy(c).start()

    def within(c, act):
        @pl.when((c >= 0) & (c < chunks))
        def _():
            act(c)

    def step(t, _):
        within(t, start_own)

        @pl.when(t == 1)
        def _():
            transpose_hidden()

        for hop in range(layers - 1, 0, -1):
            within(t - hop, lambda c: relay(c, hop))
        within(t - layers, from_across)
        within(t - layers - 1, finish)
        return 0

    lax.fori_loop(0, chunks + layers + 1, step, 0)

    def sent_all(c, wait):
        for layer in range(layers):
            @pl.when(has_up & (layer <= z))
            def _():
                wait(layer * 2 + y, UP)

            @pl.when(has_down & (layer >= z))
            def _():
                wait(layer * 2 + y, DOWN)

            wait(layer * 2 + y, ACROSS)
            wait(layer * 2 + y, SIBLING)
            wait(layer * 2 + 1 - y, SIBLING)

    def drain(c, _):
        sent_all(c, lambda origin, way: rows_copy(c, core, origin, way).wait_send())
        return 0

    lax.fori_loop(0, chunks, drain, 0)
    sent_all(0, lambda origin, way: meta_copy(core, origin, way).wait_send())
    for c in range(max(chunks - 2, 0), chunks):
        out_copy(c).wait()


def gather_shards(cotangent, expert_ids, gate_probs, seq_ids, hidden_saved):
    owners = lax.axis_size("expert")
    tok_dev, depth = cotangent.shape
    slots, ffw = hidden_saved.shape[1:]
    cap_rows = slots // owners
    seq_count = tok_dev * owners // SEQ_AVG + 2
    layers = owners // 4
    chunks = CHUNKS
    width = depth // chunks
    top = expert_ids.shape[1]
    meta = jnp.concatenate(
        [
            expert_ids.T.astype(jnp.float32),
            gate_probs.T.astype(jnp.float32),
            jnp.broadcast_to(seq_ids.astype(jnp.float32)[None, :], (top, tok_dev)),
        ],
        axis=0,
    )
    return pl.pallas_call(
        functools.partial(gather_kernel, layers, cap_rows, seq_count, chunks),
        out_shape=jax.ShapeDtypeStruct((1, ffw, depth), jnp.bfloat16),
        in_specs=[
            pl.BlockSpec(memory_space=pl.ANY),
            pl.BlockSpec(memory_space=pltpu.VMEM),
            pl.BlockSpec(memory_space=pl.ANY),
        ],
        out_specs=pl.BlockSpec(memory_space=pl.ANY),
        scratch_shapes=[
            pltpu.VMEM((chunks, 2, 2 * layers, tok_dev, width), jnp.bfloat16),
            pltpu.VMEM((2, 2 * layers, 3 * top, tok_dev), jnp.float32),
            pltpu.VMEM((slots, ffw), jnp.bfloat16),
            pltpu.VMEM((ffw, slots), jnp.bfloat16),
            pltpu.VMEM((2, 2 * layers, seq_count * cap_rows, tok_dev), jnp.bfloat16),
            pltpu.VMEM((seq_count, slots, width), jnp.bfloat16),
            pltpu.VMEM((2, ffw, width), jnp.bfloat16),
            pltpu.SemaphoreType.DMA((chunks,)),
            pltpu.SemaphoreType.DMA,
            pltpu.SemaphoreType.DMA((2,)),
            pltpu.SemaphoreType.DMA((chunks, 2 * layers, 4)),
            pltpu.SemaphoreType.DMA((chunks, 2, 2 * layers)),
            pltpu.SemaphoreType.DMA((2 * layers, 4)),
            pltpu.SemaphoreType.DMA((2, 2 * layers)),
        ],
        cost_estimate=pl.CostEstimate(
            flops=2 * seq_count * slots * ffw * depth,
            bytes_accessed=2 * depth * (ffw + tok_dev) + 2 * slots * ffw,
            transcendentals=0,
        ),
        compiler_params=pltpu.CompilerParams(
            collective_id=0, has_side_effects=True, vmem_limit_bytes=52 * 1024 * 1024
        ),
    )(cotangent, meta, hidden_saved)


def parts(cotangent, expert_ids, gate_probs, seq_ids, hidden_saved):
    owners = lax.axis_size("expert")
    cap_rows = hidden_saved.shape[1] // owners
    gathers = owners == 16 and cap_rows % 16 == 0 and 2 * cap_rows > expert_ids.shape[0]
    plan = gather_shards if gathers else shards
    return plan(cotangent, expert_ids, gate_probs, seq_ids, hidden_saved)


def solution(mesh):
    return jax.shard_map(
        parts,
        mesh=mesh,
        in_specs=(
            P(("groups", "expert"), None),
            P(("groups", "expert"), None),
            P(("groups", "expert"), None),
            P(("groups", "expert")),
            P(("groups", "expert"), None, None),
        ),
        out_specs=P(("groups", "expert"), None, None),
        check_vma=False,
    )
```

```python
import functools

import jax
import jax.numpy as jnp
from jax import lax
from jax.experimental import pallas as pl
from jax.experimental.pallas import tpu as pltpu
from jax.sharding import PartitionSpec as P

SEQ_AVG = 8192
CHUNKS = 8
STRIP = 16
LEAD = 1


def fisher_columns(arrived, hidden_rows, seq_table, seq_count, window):
    owners, cap_rows = seq_table.shape
    flat_rows = arrived.reshape(owners * cap_rows, arrived.shape[-1])
    flat_seq = seq_table.reshape(-1)
    block_last = lax.cummax(jnp.max(seq_table, axis=1), axis=0)
    span = window * cap_rows

    def one_sequence(sequence, totals):
        first_block = jnp.sum((block_last < sequence).astype(jnp.int32))
        offset = first_block * cap_rows
        hidden_part = lax.dynamic_slice_in_dim(hidden_rows, offset, span, 0)
        row_part = lax.dynamic_slice_in_dim(flat_rows, offset, span, 0)
        seq_part = lax.dynamic_slice_in_dim(flat_seq, offset, span, 0)
        chosen = jnp.where(
            (seq_part == sequence)[:, None], hidden_part, jnp.zeros_like(hidden_part)
        )
        grad_part = lax.dot_general(
            chosen, row_part, (((0,), (0,)), ((), ())), preferred_element_type=jnp.float32
        )
        return totals + grad_part * grad_part

    empty = jnp.zeros((hidden_rows.shape[1], arrived.shape[-1]), jnp.float32)
    totals = lax.fori_loop(0, seq_count, one_sequence, empty)
    return totals.astype(jnp.bfloat16)


def shards(cotangent, expert_ids, gate_probs, seq_ids, hidden_saved):
    owners = lax.axis_size("expert")
    tok_dev = expert_ids.shape[0]
    cap_rows = hidden_saved.shape[1] // owners
    total_tokens = tok_dev * owners
    seq_count = total_tokens // SEQ_AVG + 2
    seq_longest = min(SEQ_AVG * 9 // 8, total_tokens - seq_count + 1)
    window = min(seq_longest // tok_dev + 2, owners)
    expert_iota = jnp.arange(owners, dtype=jnp.int32)
    per_expert = jnp.sum(
        (expert_ids[:, :, None] == expert_iota[None, None, :]).astype(jnp.int32), axis=1
    )
    arrival = jnp.cumsum(per_expert, axis=0) - per_expert
    pair_rank = jnp.take_along_axis(arrival, expert_ids, axis=1)
    pair_slot = expert_ids * cap_rows + pair_rank
    slot_iota = jnp.arange(owners * cap_rows, dtype=jnp.int32)
    placed = slot_iota[:, None, None] == pair_slot[None, :, :]
    weights = jnp.where(placed, gate_probs.astype(jnp.float32)[None, :, :], 0.0)
    dispatch = jnp.sum(weights, axis=2).astype(jnp.bfloat16)
    outgoing = jnp.dot(dispatch, cotangent, preferred_element_type=jnp.float32).astype(jnp.bfloat16)
    outgoing = outgoing.reshape(owners, cap_rows, cotangent.shape[1])
    seq_spread = jnp.broadcast_to(seq_ids[:, None], expert_ids.shape)
    outgoing_seq = (
        jnp.full((owners, cap_rows), -1, jnp.int32).at[expert_ids, pair_rank].set(seq_spread)
    )
    seq_table = lax.all_to_all(outgoing_seq, "expert", split_axis=0, concat_axis=0, tiled=True)
    hidden_rows = hidden_saved[0]
    fisher = fisher_columns(
        lax.all_to_all(outgoing, "expert", split_axis=0, concat_axis=0, tiled=True),
        hidden_rows,
        seq_table,
        seq_count,
        window,
    )
    return fisher[None]


MESH = pl.DeviceIdType.MESH
UP, DOWN, ACROSS, SIBLING = range(4)


def gather_kernel(
    layers, cap_rows, seq_count, chunks,
    cot_ref, ids_ref, gate_ref, seq_ref, hidden_ref, out_ref,
    rows_all, meta_all, hidden_buf, hidden_t, pick_w, slot_rows, stage,
    own_sem, hidden_sem, out_sem, send_sem, recv_sem, strip_send, strip_recv, meta_send, meta_recv,
):
    places = 2 * layers
    tok_dev, width = rows_all.shape[3:]
    main = tok_dev - STRIP
    ffw = hidden_t.shape[0]
    me = lax.axis_index("expert")
    core = lax.rem(me, 2)
    place = me // 2
    y = lax.rem(place, 2)
    z = place // 2
    has_up, has_down = z < layers - 1, z > 0
    device = {UP: me + 4, DOWN: me - 4, ACROSS: me + 2 - 4 * y, SIBLING: me + 1 - 2 * core}

    def own_copy(c):
        columns = pl.ds(pl.multiple_of(c * width, width), width)
        return pltpu.make_async_copy(cot_ref.at[:, columns], rows_all.at[c, core, place], own_sem.at[c])

    def strip_copy(c, origin, way):
        strip = rows_all.at[c, core, origin, pl.ds(main, STRIP)]
        return pltpu.make_async_remote_copy(
            src_ref=strip,
            dst_ref=strip,
            send_sem=strip_send.at[c, origin // 2, way],
            recv_sem=strip_recv.at[c, origin // 2],
            device_id={"expert": device[way]},
            device_id_type=MESH,
        )

    def rows_copy(c, plane, origin, way, most=False):
        piece = rows_all.at[c, plane, origin, pl.ds(0, main)] if most else rows_all.at[c, plane, origin]
        return pltpu.make_async_remote_copy(
            src_ref=piece,
            dst_ref=piece,
            send_sem=send_sem.at[c, origin, way],
            recv_sem=recv_sem.at[c, plane, origin],
            device_id={"expert": device[way]},
            device_id_type=MESH,
        )

    def meta_copy(plane, origin, way):
        return pltpu.make_async_remote_copy(
            src_ref=meta_all.at[plane, origin],
            dst_ref=meta_all.at[plane, origin],
            send_sem=meta_send.at[origin, way],
            recv_sem=meta_recv.at[plane, origin],
            device_id={"expert": device[way]},
            device_id_type=MESH,
        )

    def out_copy(c):
        columns = pl.ds(pl.multiple_of(c * width, width), width)
        slot = lax.rem(c, 2)
        return pltpu.make_async_copy(stage.at[slot], out_ref.at[0, :, columns], out_sem.at[slot])

    def send(c, origin, ways, most=False):
        @pl.when(jnp.int32(c) == 0)
        def _():
            for way in ways:
                meta_copy(core, origin, way).start()

        for way in ways:
            rows_copy(c, core, origin, way, most).start()

    def arrive(c, plane, origin, most=False):
        @pl.when(c == 0)
        def _():
            meta_copy(plane, origin, SIBLING).wait_recv()

        rows_copy(c, plane, origin, SIBLING, most).wait_recv()

    hidden_copy = pltpu.make_async_copy(hidden_ref.at[0], hidden_buf, hidden_sem)
    for c in range(chunks):
        own_copy(c).start()
    hidden_copy.start()
    top = ids_ref.shape[0]
    meta_all[core, place, 0:top] = ids_ref[...].astype(jnp.float32)
    meta_all[core, place, top:2 * top] = gate_ref[...].astype(jnp.float32)
    meta_all[core, place, 2 * top:3 * top] = jnp.broadcast_to(
        seq_ref[...].astype(jnp.float32), (top, tok_dev)
    )

    barrier = pltpu.get_barrier_semaphore()
    for way in (ACROSS, SIBLING):
        pl.semaphore_signal(barrier, inc=1, device_id={"expert": device[way]}, device_id_type=MESH)
    for way, there in ((UP, has_up), (DOWN, has_down)):
        @pl.when(there)
        def _():
            pl.semaphore_signal(barrier, inc=1, device_id={"expert": device[way]}, device_id_type=MESH)
    pl.semaphore_wait(barrier, 2 + has_up.astype(jnp.int32) + has_down.astype(jnp.int32))

    def start_own(c):
        own_copy(c).wait()

        @pl.when(has_up)
        def _():
            send(c, place, (UP,))

        @pl.when(has_down)
        def _():
            send(c, place, (DOWN,))

        send(c, place, (ACROSS, SIBLING))

    def relay(c, hop):
        for source, there, onward, way in (
            (z - hop, z >= hop, has_up, UP),
            (z + hop, z + hop < layers, has_down, DOWN),
        ):
            @pl.when(there)
            def _():
                origin = source * 2 + y
                arrive(c, core, origin)

                @pl.when(onward)
                def _():
                    send(c, origin, (way,))

                send(c, origin, (ACROSS,), True)
                send(c, origin, (SIBLING,))

    def same_layer(c):
        origin = z * 2 + 1 - y
        arrive(c, core, origin)
        for there, way in ((has_up, UP), (has_down, DOWN)):
            @pl.when(there)
            def _():
                strip_copy(c, origin, way).start()

        send(c, origin, (SIBLING,))

    def relay_strip(c, hop):
        for source, there, onward, way in (
            (z - hop, z >= hop, has_up, UP),
            (z + hop, z + hop < layers, has_down, DOWN),
        ):
            @pl.when(there)
            def _():
                origin = source * 2 + 1 - y
                strip_copy(c, origin, way).wait_recv()

                @pl.when(onward)
                def _():
                    strip_copy(c, origin, way).start()

    def from_across(c):
        for layer in range(layers):
            @pl.when(z != layer)
            def _():
                origin = layer * 2 + 1 - y
                arrive(c, core, origin, True)
                send(c, origin, (SIBLING,))

    def transpose_hidden():
        hidden_copy.wait()

        def one(i, _):
            rows = pl.ds(pl.multiple_of(i * 128, 128), 128)
            hidden_t[:, rows] = hidden_buf[rows, :].T
            return 0

        lax.fori_loop(0, hidden_buf.shape[0] // 128, one, 0)

    def prepare():
        earlier = lax.broadcasted_iota(jnp.int32, (tok_dev, tok_dev), 0) < lax.broadcasted_iota(
            jnp.int32, (tok_dev, tok_dev), 1
        )
        earlier = earlier.astype(jnp.float32).astype(jnp.bfloat16)
        slots = lax.broadcasted_iota(jnp.int32, (cap_rows, tok_dev), 0).astype(jnp.float32)
        expert = me.astype(jnp.float32)
        top = meta_all.shape[2] // 3
        for plane in range(2):
            table = meta_all[plane]
            named = table[:, :top, :] == expert
            routed = jnp.sum(jnp.where(named, 1.0, 0.0), axis=1)
            gate = jnp.sum(jnp.where(named, table[:, top:2 * top, :], 0.0), axis=1)
            rank = jnp.dot(routed.astype(jnp.bfloat16), earlier, preferred_element_type=jnp.float32)
            for origin in range(places):
                here = routed[origin:origin + 1] > 0
                sequence = table[origin, 2 * top:2 * top + 1, :]
                for s in range(seq_count):
                    spot = jnp.where(here & (sequence == float(s)), rank[origin:origin + 1], -1.0)
                    weight = jnp.where(slots == spot, gate[origin:origin + 1], 0.0)
                    pick_w[plane, origin, s * cap_rows:(s + 1) * cap_rows, :] = weight.astype(jnp.bfloat16)

    def finish(c):
        for origin in range(places):
            arrive(c, 1 - core, origin)

        @pl.when(c == 0)
        def _():
            prepare()

        def dispatch(origin, _):
            for plane in range(2):
                sent = jnp.dot(
                    pick_w[plane, origin], rows_all[c, plane, origin], preferred_element_type=jnp.float32
                ).astype(jnp.bfloat16)
                first = pl.multiple_of((origin * 2 + plane) * cap_rows, 16)
                for s in range(seq_count):
                    slot_rows[s, pl.ds(first, cap_rows), :] = sent[s * cap_rows:(s + 1) * cap_rows]
            return 0

        lax.fori_loop(0, places, dispatch, 0)

        @pl.when(c >= 2)
        def _():
            out_copy(c - 2).wait()

        slot = lax.rem(c, 2)
        wide = 256

        def squares(n, _):
            part = pl.ds(pl.multiple_of(n * wide, wide), wide)
            total = None
            for s in range(seq_count):
                grad = jnp.dot(hidden_t[...], slot_rows[s, :, part], preferred_element_type=jnp.float32)
                total = grad * grad if total is None else total + grad * grad
            stage[slot, :, part] = total.astype(jnp.bfloat16)
            return 0

        lax.fori_loop(0, width // wide, squares, 0)
        out_copy(c).start()

    def within(c, act):
        @pl.when((c >= 0) & (c < chunks))
        def _():
            act(c)

    def step(t, _):
        within(t + LEAD, start_own)

        @pl.when(t == 1)
        def _():
            transpose_hidden()

        for hop in range(layers - 1, 0, -1):
            within(t - hop, lambda c: relay(c, hop))
        within(t - 1, same_layer)
        for hop in range(layers - 1, 0, -1):
            within(t - 1 - hop, lambda c: relay_strip(c, hop))
        within(t - layers, from_across)
        within(t - layers, finish)
        return 0

    for c in range(LEAD):
        start_own(c)
    lax.fori_loop(0, chunks + layers, step, 0)

    def sent_all(wait, wait_strip):
        for layer in range(layers):
            @pl.when(has_up & (layer <= z))
            def _():
                wait(layer * 2 + y, UP)
                wait_strip(layer * 2 + 1 - y, UP)

            @pl.when(has_down & (layer >= z))
            def _():
                wait(layer * 2 + y, DOWN)
                wait_strip(layer * 2 + 1 - y, DOWN)

            @pl.when(z == layer)
            def _():
                wait(layer * 2 + y, ACROSS)

            @pl.when(z != layer)
            def _():
                wait(layer * 2 + y, ACROSS, True)

            wait(layer * 2 + y, SIBLING)
            wait(layer * 2 + 1 - y, SIBLING)

    def drain(c, _):
        sent_all(
            lambda origin, way, most=False: rows_copy(c, core, origin, way, most).wait_send(),
            lambda origin, way: strip_copy(c, origin, way).wait_send(),
        )
        return 0

    lax.fori_loop(0, chunks, drain, 0)
    sent_all(
        lambda origin, way, most=False: meta_copy(core, origin, way).wait_send(),
        lambda origin, way: None,
    )
    for c in range(max(chunks - 2, 0), chunks):
        out_copy(c).wait()


def gather_shards(cotangent, expert_ids, gate_probs, seq_ids, hidden_saved):
    owners = lax.axis_size("expert")
    tok_dev, depth = cotangent.shape
    slots, ffw = hidden_saved.shape[1:]
    cap_rows = slots // owners
    seq_count = tok_dev * owners // SEQ_AVG + 2
    layers = owners // 4
    chunks = CHUNKS
    width = depth // chunks
    top = expert_ids.shape[1]
    return pl.pallas_call(
        functools.partial(gather_kernel, layers, cap_rows, seq_count, chunks),
        out_shape=jax.ShapeDtypeStruct((1, ffw, depth), jnp.bfloat16),
        in_specs=[
            pl.BlockSpec(memory_space=pl.ANY),
            pl.BlockSpec(memory_space=pltpu.VMEM),
            pl.BlockSpec(memory_space=pltpu.VMEM),
            pl.BlockSpec(memory_space=pltpu.VMEM),
            pl.BlockSpec(memory_space=pl.ANY),
        ],
        out_specs=pl.BlockSpec(memory_space=pl.ANY),
        scratch_shapes=[
            pltpu.VMEM((chunks, 2, 2 * layers, tok_dev, width), jnp.bfloat16),
            pltpu.VMEM((2, 2 * layers, 3 * top, tok_dev), jnp.float32),
            pltpu.VMEM((slots, ffw), jnp.bfloat16),
            pltpu.VMEM((ffw, slots), jnp.bfloat16),
            pltpu.VMEM((2, 2 * layers, seq_count * cap_rows, tok_dev), jnp.bfloat16),
            pltpu.VMEM((seq_count, slots, width), jnp.bfloat16),
            pltpu.VMEM((2, ffw, width), jnp.bfloat16),
            pltpu.SemaphoreType.DMA((chunks,)),
            pltpu.SemaphoreType.DMA,
            pltpu.SemaphoreType.DMA((2,)),
            pltpu.SemaphoreType.DMA((chunks, 2 * layers, 4)),
            pltpu.SemaphoreType.DMA((chunks, 2, 2 * layers)),
            pltpu.SemaphoreType.DMA((chunks, layers, 2)),
            pltpu.SemaphoreType.DMA((chunks, layers)),
            pltpu.SemaphoreType.DMA((2 * layers, 4)),
            pltpu.SemaphoreType.DMA((2, 2 * layers)),
        ],
        cost_estimate=pl.CostEstimate(
            flops=2 * seq_count * slots * ffw * depth,
            bytes_accessed=2 * depth * (ffw + tok_dev) + 2 * slots * ffw,
            transcendentals=0,
        ),
        compiler_params=pltpu.CompilerParams(
            collective_id=0, has_side_effects=True, vmem_limit_bytes=60 * 1024 * 1024
        ),
    )(cotangent, expert_ids.T, gate_probs.T, seq_ids[None, :], hidden_saved)


def parts(cotangent, expert_ids, gate_probs, seq_ids, hidden_saved):
    owners = lax.axis_size("expert")
    cap_rows = hidden_saved.shape[1] // owners
    gathers = owners == 16 and cap_rows % 16 == 0 and 2 * cap_rows > expert_ids.shape[0]
    plan = gather_shards if gathers else shards
    return plan(cotangent, expert_ids, gate_probs, seq_ids, hidden_saved)


def solution(mesh):
    return jax.shard_map(
        parts,
        mesh=mesh,
        in_specs=(
            P(("groups", "expert"), None),
            P(("groups", "expert"), None),
            P(("groups", "expert"), None),
            P(("groups", "expert")),
            P(("groups", "expert"), None, None),
        ),
        out_specs=P(("groups", "expert"), None, None),
        check_vma=False,
    )
```

```python
import functools

import jax
import jax.numpy as jnp
from jax import lax
from jax.experimental import pallas as pl
from jax.experimental.pallas import tpu as pltpu
from jax.sharding import PartitionSpec as P

SEQ_AVG = 8192
CHUNKS = 8
STRIP = 16
LEAD = 1


def fisher_columns(arrived, hidden_rows, seq_table, seq_count, window):
    owners, cap_rows = seq_table.shape
    flat_rows = arrived.reshape(owners * cap_rows, arrived.shape[-1])
    flat_seq = seq_table.reshape(-1)
    block_last = lax.cummax(jnp.max(seq_table, axis=1), axis=0)
    span = window * cap_rows

    def one_sequence(sequence, totals):
        first_block = jnp.sum((block_last < sequence).astype(jnp.int32))
        offset = first_block * cap_rows
        hidden_part = lax.dynamic_slice_in_dim(hidden_rows, offset, span, 0)
        row_part = lax.dynamic_slice_in_dim(flat_rows, offset, span, 0)
        seq_part = lax.dynamic_slice_in_dim(flat_seq, offset, span, 0)
        chosen = jnp.where(
            (seq_part == sequence)[:, None], hidden_part, jnp.zeros_like(hidden_part)
        )
        grad_part = lax.dot_general(
            chosen, row_part, (((0,), (0,)), ((), ())), preferred_element_type=jnp.float32
        )
        return totals + grad_part * grad_part

    empty = jnp.zeros((hidden_rows.shape[1], arrived.shape[-1]), jnp.float32)
    totals = lax.fori_loop(0, seq_count, one_sequence, empty)
    return totals.astype(jnp.bfloat16)


def shards(cotangent, expert_ids, gate_probs, seq_ids, hidden_saved):
    owners = lax.axis_size("expert")
    tok_dev = expert_ids.shape[0]
    cap_rows = hidden_saved.shape[1] // owners
    total_tokens = tok_dev * owners
    seq_count = total_tokens // SEQ_AVG + 2
    seq_longest = min(SEQ_AVG * 9 // 8, total_tokens - seq_count + 1)
    window = min(seq_longest // tok_dev + 2, owners)
    expert_iota = jnp.arange(owners, dtype=jnp.int32)
    per_expert = jnp.sum(
        (expert_ids[:, :, None] == expert_iota[None, None, :]).astype(jnp.int32), axis=1
    )
    arrival = jnp.cumsum(per_expert, axis=0) - per_expert
    pair_rank = jnp.take_along_axis(arrival, expert_ids, axis=1)
    pair_slot = expert_ids * cap_rows + pair_rank
    slot_iota = jnp.arange(owners * cap_rows, dtype=jnp.int32)
    placed = slot_iota[:, None, None] == pair_slot[None, :, :]
    weights = jnp.where(placed, gate_probs.astype(jnp.float32)[None, :, :], 0.0)
    dispatch = jnp.sum(weights, axis=2).astype(jnp.bfloat16)
    outgoing = jnp.dot(dispatch, cotangent, preferred_element_type=jnp.float32).astype(jnp.bfloat16)
    outgoing = outgoing.reshape(owners, cap_rows, cotangent.shape[1])
    seq_spread = jnp.broadcast_to(seq_ids[:, None], expert_ids.shape)
    outgoing_seq = (
        jnp.full((owners, cap_rows), -1, jnp.int32).at[expert_ids, pair_rank].set(seq_spread)
    )
    seq_table = lax.all_to_all(outgoing_seq, "expert", split_axis=0, concat_axis=0, tiled=True)
    hidden_rows = hidden_saved[0]
    fisher = fisher_columns(
        lax.all_to_all(outgoing, "expert", split_axis=0, concat_axis=0, tiled=True),
        hidden_rows,
        seq_table,
        seq_count,
        window,
    )
    return fisher[None]


MESH = pl.DeviceIdType.MESH
UP, DOWN, ACROSS, SIBLING = range(4)


def gather_kernel(
    layers, cap_rows, seq_count, chunks,
    cot_ref, ids_ref, gate_ref, seq_ref, hidden_ref, out_ref,
    rows_all, meta_all, hidden_buf, hidden_t, pick_w, slot_rows, stage,
    own_sem, hidden_sem, out_sem, send_sem, recv_sem, strip_send, strip_recv, meta_send, meta_recv,
):
    places = 2 * layers
    tok_dev, width = rows_all.shape[3:]
    main = tok_dev - STRIP
    ffw = hidden_t.shape[0]
    me = lax.axis_index("expert")
    core = lax.rem(me, 2)
    place = me // 2
    y = lax.rem(place, 2)
    z = place // 2
    has_up, has_down = z < layers - 1, z > 0
    device = {UP: me + 4, DOWN: me - 4, ACROSS: me + 2 - 4 * y, SIBLING: me + 1 - 2 * core}

    def own_copy(c):
        columns = pl.ds(pl.multiple_of(c * width, width), width)
        return pltpu.make_async_copy(cot_ref.at[:, columns], rows_all.at[c, core, place], own_sem.at[c])

    def strip_copy(c, origin, way):
        strip = rows_all.at[c, core, origin, pl.ds(main, STRIP)]
        return pltpu.make_async_remote_copy(
            src_ref=strip,
            dst_ref=strip,
            send_sem=strip_send.at[c, origin // 2, way],
            recv_sem=strip_recv.at[c, origin // 2],
            device_id={"expert": device[way]},
            device_id_type=MESH,
        )

    def rows_copy(c, plane, origin, way, most=False):
        piece = rows_all.at[c, plane, origin, pl.ds(0, main)] if most else rows_all.at[c, plane, origin]
        return pltpu.make_async_remote_copy(
            src_ref=piece,
            dst_ref=piece,
            send_sem=send_sem.at[c, origin, way],
            recv_sem=recv_sem.at[c, plane, origin],
            device_id={"expert": device[way]},
            device_id_type=MESH,
        )

    def meta_copy(plane, origin, way):
        return pltpu.make_async_remote_copy(
            src_ref=meta_all.at[plane, origin],
            dst_ref=meta_all.at[plane, origin],
            send_sem=meta_send.at[origin, way],
            recv_sem=meta_recv.at[plane, origin],
            device_id={"expert": device[way]},
            device_id_type=MESH,
        )

    def out_copy(c):
        columns = pl.ds(pl.multiple_of(c * width, width), width)
        slot = lax.rem(c, 2)
        return pltpu.make_async_copy(stage.at[slot], out_ref.at[0, :, columns], out_sem.at[slot])

    def send(c, origin, ways, most=False):
        @pl.when(jnp.int32(c) == 0)
        def _():
            for way in ways:
                meta_copy(core, origin, way).start()

        for way in ways:
            rows_copy(c, core, origin, way, most).start()

    def arrive(c, plane, origin, most=False):
        @pl.when(c == 0)
        def _():
            meta_copy(plane, origin, SIBLING).wait_recv()

        rows_copy(c, plane, origin, SIBLING, most).wait_recv()

    hidden_copy = pltpu.make_async_copy(hidden_ref.at[0], hidden_buf, hidden_sem)
    for c in range(chunks):
        own_copy(c).start()
    hidden_copy.start()
    top = ids_ref.shape[0]
    meta_all[core, place, 0:top] = ids_ref[...].astype(jnp.float32)
    meta_all[core, place, top:2 * top] = gate_ref[...].astype(jnp.float32)
    meta_all[core, place, 2 * top:3 * top] = jnp.broadcast_to(
        seq_ref[...].astype(jnp.float32), (top, tok_dev)
    )

    barrier = pltpu.get_barrier_semaphore()
    for way in (ACROSS, SIBLING):
        pl.semaphore_signal(barrier, inc=1, device_id={"expert": device[way]}, device_id_type=MESH)
    for way, there in ((UP, has_up), (DOWN, has_down)):
        @pl.when(there)
        def _():
            pl.semaphore_signal(barrier, inc=1, device_id={"expert": device[way]}, device_id_type=MESH)
    pl.semaphore_wait(barrier, 2 + has_up.astype(jnp.int32) + has_down.astype(jnp.int32))

    def start_own(c):
        own_copy(c).wait()

        @pl.when(has_up)
        def _():
            send(c, place, (UP,))

        @pl.when(has_down)
        def _():
            send(c, place, (DOWN,))

        send(c, place, (ACROSS, SIBLING))

    def relay(c, hop):
        for source, there, onward, way in (
            (z - hop, z >= hop, has_up, UP),
            (z + hop, z + hop < layers, has_down, DOWN),
        ):
            @pl.when(there)
            def _():
                origin = source * 2 + y
                arrive(c, core, origin)

                @pl.when(onward)
                def _():
                    send(c, origin, (way,))

                send(c, origin, (ACROSS,), True)
                send(c, origin, (SIBLING,))

    def same_layer(c):
        origin = z * 2 + 1 - y
        arrive(c, core, origin)
        for there, way in ((has_up, UP), (has_down, DOWN)):
            @pl.when(there)
            def _():
                strip_copy(c, origin, way).start()

        send(c, origin, (SIBLING,))

    def relay_strip(c, hop):
        for source, there, onward, way in (
            (z - hop, z >= hop, has_up, UP),
            (z + hop, z + hop < layers, has_down, DOWN),
        ):
            @pl.when(there)
            def _():
                origin = source * 2 + 1 - y
                strip_copy(c, origin, way).wait_recv()

                @pl.when(onward)
                def _():
                    strip_copy(c, origin, way).start()

    def from_across(c):
        for layer in range(layers):
            @pl.when(z != layer)
            def _():
                origin = layer * 2 + 1 - y
                arrive(c, core, origin, True)
                send(c, origin, (SIBLING,))

    def transpose_hidden():
        hidden_copy.wait()

        def one(i, _):
            rows = pl.ds(pl.multiple_of(i * 128, 128), 128)
            hidden_t[:, rows] = hidden_buf[rows, :].T
            return 0

        lax.fori_loop(0, hidden_buf.shape[0] // 128, one, 0)

    def prepare():
        earlier = lax.broadcasted_iota(jnp.int32, (tok_dev, tok_dev), 0) < lax.broadcasted_iota(
            jnp.int32, (tok_dev, tok_dev), 1
        )
        earlier = earlier.astype(jnp.float32).astype(jnp.bfloat16)
        slots = lax.broadcasted_iota(jnp.int32, (cap_rows, tok_dev), 0).astype(jnp.float32)
        expert = me.astype(jnp.float32)
        top = meta_all.shape[2] // 3
        for plane in range(2):
            table = meta_all[plane]
            named = table[:, :top, :] == expert
            routed = jnp.sum(jnp.where(named, 1.0, 0.0), axis=1)
            gate = jnp.sum(jnp.where(named, table[:, top:2 * top, :], 0.0), axis=1)
            rank = jnp.dot(routed.astype(jnp.bfloat16), earlier, preferred_element_type=jnp.float32)
            for origin in range(places):
                here = routed[origin:origin + 1] > 0
                sequence = table[origin, 2 * top:2 * top + 1, :]
                for s in range(seq_count):
                    spot = jnp.where(here & (sequence == float(s)), rank[origin:origin + 1], -1.0)
                    weight = jnp.where(slots == spot, gate[origin:origin + 1], 0.0)
                    pick_w[plane, origin, s * cap_rows:(s + 1) * cap_rows, :] = weight.astype(jnp.bfloat16)

    def finish(c):
        for origin in range(places):
            arrive(c, 1 - core, origin)

        @pl.when(c == 0)
        def _():
            prepare()

        def dispatch(origin, _):
            for plane in range(2):
                sent = jnp.dot(
                    pick_w[plane, origin], rows_all[c, plane, origin], preferred_element_type=jnp.float32
                ).astype(jnp.bfloat16)
                first = pl.multiple_of((origin * 2 + plane) * cap_rows, 16)
                for s in range(seq_count):
                    slot_rows[s, pl.ds(first, cap_rows), :] = sent[s * cap_rows:(s + 1) * cap_rows]
            return 0

        lax.fori_loop(0, places, dispatch, 0, unroll=4)

        @pl.when(c >= 2)
        def _():
            out_copy(c - 2).wait()

        slot = lax.rem(c, 2)
        wide = 256

        def squares(n, _):
            part = pl.ds(pl.multiple_of(n * wide, wide), wide)
            total = None
            for s in range(seq_count):
                grad = jnp.dot(hidden_t[...], slot_rows[s, :, part], preferred_element_type=jnp.float32)
                total = grad * grad if total is None else total + grad * grad
            stage[slot, :, part] = total.astype(jnp.bfloat16)
            return 0

        lax.fori_loop(0, width // wide, squares, 0)
        out_copy(c).start()

    def within(c, act):
        @pl.when((c >= 0) & (c < chunks))
        def _():
            act(c)

    def step(t, _):
        within(t + LEAD, start_own)

        @pl.when(t == 1)
        def _():
            transpose_hidden()

        for hop in range(layers - 1, 0, -1):
            within(t - hop, lambda c: relay(c, hop))
            within(t - 1 - hop, lambda c: relay_strip(c, hop))
        within(t - 1, same_layer)
        within(t - layers, from_across)
        within(t - layers, finish)
        return 0

    for c in range(LEAD):
        start_own(c)
    lax.fori_loop(0, chunks + layers, step, 0)

    def sent_all(wait, wait_strip):
        for layer in range(layers):
            @pl.when(has_up & (layer <= z))
            def _():
                wait(layer * 2 + y, UP)
                wait_strip(layer * 2 + 1 - y, UP)

            @pl.when(has_down & (layer >= z))
            def _():
                wait(layer * 2 + y, DOWN)
                wait_strip(layer * 2 + 1 - y, DOWN)

            @pl.when(z == layer)
            def _():
                wait(layer * 2 + y, ACROSS)

            @pl.when(z != layer)
            def _():
                wait(layer * 2 + y, ACROSS, True)

            wait(layer * 2 + y, SIBLING)
            wait(layer * 2 + 1 - y, SIBLING)

    def drain(c, _):
        sent_all(
            lambda origin, way, most=False: rows_copy(c, core, origin, way, most).wait_send(),
            lambda origin, way: strip_copy(c, origin, way).wait_send(),
        )
        return 0

    lax.fori_loop(0, chunks, drain, 0)
    sent_all(
        lambda origin, way, most=False: meta_copy(core, origin, way).wait_send(),
        lambda origin, way: None,
    )
    for c in range(max(chunks - 2, 0), chunks):
        out_copy(c).wait()


def gather_shards(cotangent, expert_ids, gate_probs, seq_ids, hidden_saved):
    owners = lax.axis_size("expert")
    tok_dev, depth = cotangent.shape
    slots, ffw = hidden_saved.shape[1:]
    cap_rows = slots // owners
    seq_count = tok_dev * owners // SEQ_AVG + 2
    layers = owners // 4
    chunks = CHUNKS
    width = depth // chunks
    top = expert_ids.shape[1]
    return pl.pallas_call(
        functools.partial(gather_kernel, layers, cap_rows, seq_count, chunks),
        out_shape=jax.ShapeDtypeStruct((1, ffw, depth), jnp.bfloat16),
        in_specs=[
            pl.BlockSpec(memory_space=pl.ANY),
            pl.BlockSpec(memory_space=pltpu.VMEM),
            pl.BlockSpec(memory_space=pltpu.VMEM),
            pl.BlockSpec(memory_space=pltpu.VMEM),
            pl.BlockSpec(memory_space=pl.ANY),
        ],
        out_specs=pl.BlockSpec(memory_space=pl.ANY),
        scratch_shapes=[
            pltpu.VMEM((chunks, 2, 2 * layers, tok_dev, width), jnp.bfloat16),
            pltpu.VMEM((2, 2 * layers, 3 * top, tok_dev), jnp.float32),
            pltpu.VMEM((slots, ffw), jnp.bfloat16),
            pltpu.VMEM((ffw, slots), jnp.bfloat16),
            pltpu.VMEM((2, 2 * layers, seq_count * cap_rows, tok_dev), jnp.bfloat16),
            pltpu.VMEM((seq_count, slots, width), jnp.bfloat16),
            pltpu.VMEM((2, ffw, width), jnp.bfloat16),
            pltpu.SemaphoreType.DMA((chunks,)),
            pltpu.SemaphoreType.DMA,
            pltpu.SemaphoreType.DMA((2,)),
            pltpu.SemaphoreType.DMA((chunks, 2 * layers, 4)),
            pltpu.SemaphoreType.DMA((chunks, 2, 2 * layers)),
            pltpu.SemaphoreType.DMA((chunks, layers, 2)),
            pltpu.SemaphoreType.DMA((chunks, layers)),
            pltpu.SemaphoreType.DMA((2 * layers, 4)),
            pltpu.SemaphoreType.DMA((2, 2 * layers)),
        ],
        cost_estimate=pl.CostEstimate(
            flops=2 * seq_count * slots * ffw * depth,
            bytes_accessed=2 * depth * (ffw + tok_dev) + 2 * slots * ffw,
            transcendentals=0,
        ),
        compiler_params=pltpu.CompilerParams(
            collective_id=0, has_side_effects=True, vmem_limit_bytes=60 * 1024 * 1024
        ),
    )(cotangent, expert_ids.T, gate_probs.T, seq_ids[None, :], hidden_saved)


def parts(cotangent, expert_ids, gate_probs, seq_ids, hidden_saved):
    owners = lax.axis_size("expert")
    cap_rows = hidden_saved.shape[1] // owners
    gathers = owners == 16 and cap_rows % 16 == 0 and 2 * cap_rows > expert_ids.shape[0]
    plan = gather_shards if gathers else shards
    return plan(cotangent, expert_ids, gate_probs, seq_ids, hidden_saved)


def solution(mesh):
    return jax.shard_map(
        parts,
        mesh=mesh,
        in_specs=(
            P(("groups", "expert"), None),
            P(("groups", "expert"), None),
            P(("groups", "expert"), None),
            P(("groups", "expert")),
            P(("groups", "expert"), None, None),
        ),
        out_specs=P(("groups", "expert"), None, None),
        check_vma=False,
    )
```
